32 devices in a mesh: tm: 4 (over y, x), space: 8 (over z, core).
Axes of the slice: x: 2, y: 2, z: 4, core: 2. Of those that a mesh axis runs over, the one named last changes fastest.
Arguments:
- latent_clip: bfloat16 [8, 16, 32, 256], P('tm', 'space'), may hold values from -45 to 45
- cotangent: bfloat16 [8, 16, 32, 128], P('tm', 'space'), may hold values from -6 to 6
- conv_weight: bfloat16 [6912, 128], replicated, may hold values from -0.078125 to 0.078125
- norm_gain: float32 [256], replicated, may hold values from 0.5 to 1.5
- norm_shift: float32 [256], replicated, may hold values from -2 to 2
Outputs:
- clip_grad: bfloat16 [8, 16, 32, 256], P('tm', 'space')
- weight_grad: float32 [6912, 128], P('space')
- gain_grad: float32 [256], replicated
- shift_grad: float32 [256], replicated
The draws below stay inside these ranges and needn't reach their ends.
All inputs are finite; a program needn't handle non-finite values.
Results may differ from the reference program's by a relative error of at most 0.0029.
Values may be sent and summed in bfloat16 or wider, within the bound.
A program may use at most 64 MiB of HBM per device.

```python
import math
import jax
import jax.numpy as jnp
from jax import lax

C = 256
CO = 128
GROUPS = 32
W = 32
FRAMES = 8
ROWS = 16


def draw_latent_clip(key, part):
    keys = jax.random.split(key, 3)
    base = jnp.clip(jax.random.normal(keys[0], (FRAMES, ROWS, W, C), jnp.float32), -3.0, 3.0)
    row_scale = jnp.exp(jax.random.uniform(keys[1], (FRAMES, ROWS, 1, 1), jnp.float32, math.log(0.5), math.log(3.0)))
    channel_scale = jnp.exp(jax.random.uniform(keys[2], (C,), jnp.float32, math.log(0.7), math.log(1.5)))
    rising = 1.0 + 2.0 * jnp.arange(ROWS, dtype=jnp.float32).reshape(1, ROWS, 1, 1) / ROWS
    return (base * row_scale * channel_scale * rising).astype(jnp.bfloat16)


def block_levels(rng, dims, cuts, least, high):
    level = 1.0
    for axis_at, parts in cuts:
        heights = jax.random.uniform(jax.random.fold_in(jax.random.fold_in(rng, 6), axis_at), (parts,), jnp.float32, least / len(cuts), high / len(cuts))
        level = level * jnp.repeat(jnp.exp(heights), dims[axis_at] // parts).reshape((-1,) + (1,) * (len(dims) - 1 - axis_at))
    return level


def centred(key, shape, spread, bound, pieces=(), held_as=jnp.bfloat16):
    array = spread * jax.random.normal(key, shape, jnp.float32)
    if pieces:
        array = array * block_levels(key, shape, pieces, -0.22, 0.18)
    return jnp.clip(array, -bound, bound).astype(held_as)


def setup_inputs(seed: int = 0) -> dict:
    arg_keys = jax.random.split(jax.random.key(seed), 6)
    return {
        "latent_clip": draw_latent_clip(jax.random.fold_in(arg_keys[5], 71), 0),
        "cotangent": centred(arg_keys[1], (FRAMES, ROWS, W, CO), 1.0, 6.0, ((0, 4), (1, 8))),
        "conv_weight": centred(arg_keys[2], (27 * C, CO), (27 * C) ** -0.5, 0.078125),
        "norm_gain": jnp.clip(jax.random.uniform(arg_keys[3], (C,), jnp.float32, 0.5, 1.5), 0.5, 1.5),
        "norm_shift": centred(arg_keys[4], (C,), 0.5, 2.0, (), jnp.float32),
    }


def silu_slope(activation):
    sigma = jax.nn.sigmoid(activation)
    return sigma * (1.0 + activation * (1.0 - sigma))

def reference(latent_clip, cotangent, conv_weight, norm_gain, norm_shift):
    frame_total, row_total, col_total, channels = latent_clip.shape
    out_channels = cotangent.shape[-1]
    width_group = channels // GROUPS
    group_count = frame_total * row_total * col_total * width_group
    values = latent_clip.astype(jnp.float32).reshape(frame_total, row_total, col_total, GROUPS, width_group)
    group_mean = lax.optimization_barrier(jnp.sum(values, axis=(0, 1, 2, 4))) / group_count
    centered = values - group_mean[:, None]
    group_var = lax.optimization_barrier(jnp.sum(centered * centered, axis=(0, 1, 2, 4))) / group_count
    inv_std = lax.rsqrt(group_var + 1e-06)
    normed = (centered * inv_std[:, None]).reshape(frame_total, row_total, col_total, channels)
    activation = normed * norm_gain + norm_shift
    hidden = jax.nn.silu(activation).astype(jnp.bfloat16)
    padded = jnp.pad(hidden, ((2, 0), (1, 1), (1, 1), (0, 0)))
    cell_count = frame_total * row_total * col_total
    upstream = cotangent.reshape(cell_count, out_channels)
    tap_grads = []
    for tap_time in range(3):
        for tap_row in range(3):
            for tap_col in range(3):
                piece = padded[tap_time:tap_time + frame_total, tap_row:tap_row + row_total, tap_col:tap_col + col_total]
                piece = piece.reshape(cell_count, channels)
                tap_grads.append(lax.dot_general(piece, upstream, (((0,), (0,)), ((), ())), preferred_element_type=jnp.float32))
    weight_grad = jnp.concatenate(tap_grads, axis=0)
    kernel = conv_weight.reshape(3, 3, 3, channels, out_channels)
    grad_pad = jnp.pad(cotangent, ((0, 2), (1, 1), (1, 1), (0, 0)))
    hidden_grad = jnp.zeros((cell_count, channels), jnp.float32)
    for tap_time in range(3):
        for tap_row in range(3):
            for tap_col in range(3):
                piece = grad_pad[2 - tap_time:2 - tap_time + frame_total, 2 - tap_row:2 - tap_row + row_total, 2 - tap_col:2 - tap_col + col_total]
                piece = piece.reshape(cell_count, out_channels)
                hidden_grad = hidden_grad + jnp.dot(piece, kernel[tap_time, tap_row, tap_col].T, preferred_element_type=jnp.float32)
    hidden_grad = hidden_grad.reshape(frame_total, row_total, col_total, channels)
    activation_grad = hidden_grad * silu_slope(activation)
    gain_grad = lax.optimization_barrier(jnp.sum(activation_grad * normed, axis=(0, 1, 2)))
    shift_grad = lax.optimization_barrier(jnp.sum(activation_grad, axis=(0, 1, 2)))
    first = lax.optimization_barrier(jnp.sum((norm_gain * shift_grad).reshape(GROUPS, width_group), axis=1))
    second = lax.optimization_barrier(jnp.sum((norm_gain * gain_grad).reshape(GROUPS, width_group), axis=1))
    scaled = (activation_grad * norm_gain).reshape(frame_total, row_total, col_total, GROUPS, width_group)
    normed_groups = normed.reshape(frame_total, row_total, col_total, GROUPS, width_group)
    clip_grad = inv_std[:, None] * (scaled - first[:, None] / group_count - normed_groups * second[:, None] / group_count)
    clip_grad = clip_grad.reshape(frame_total, row_total, col_total, channels).astype(jnp.bfloat16)
    return (clip_grad, weight_grad, gain_grad, shift_grad)
```

```python
import functools

import jax
import jax.numpy as jnp
from jax import lax
from jax.experimental import pallas as pl
from jax.experimental.pallas import tpu as pltpu
from jax.sharding import PartitionSpec as P

GROUPS = 32
UNIT = 32


def fused_kernel(
    T, S, shard, chunk,
    x_ref, c_ref, w_hbm, gain_ref, shift_ref,
    clip_ref, wg_out, gg_ref, sg_ref,
    w_ref, xg, cg, g3, st1, st2, gr1, gr2, hg, ht, wg, pbuf, sbuf, rbuf, abuf,
    send_sem, recv_sem, w_sem,
):
    F, R, W, C = x_ref.shape
    O = c_ref.shape[-1]
    Z = S // 2
    cells = F * R * W
    j = lax.axis_index("tm")
    s = lax.axis_index("space")
    z = s // 2
    core = s % 2
    wrap_s = lambda v: lax.rem(v + S, S)
    wrap_j = lambda v: lax.rem(v + T, T)

    w_copy = pltpu.make_async_copy(w_hbm, w_ref, w_sem)
    w_copy.start()

    peers = []
    for dj in range(T):
        for ds in range(S):
            if (dj, ds) != (0, 0) and (dj == 0 or ds in (0, 1, S - 1)):
                peers.append((wrap_j(j + dj), wrap_s(s + ds)))
    barrier = pltpu.get_barrier_semaphore()
    for peer in peers:
        pl.semaphore_signal(barrier, inc=1, device_id=peer, device_id_type=pl.DeviceIdType.MESH)

    counter = [0]

    def remote(src, dst, peer):
        k = counter[0]
        counter[0] += 1
        copy = pltpu.make_async_remote_copy(
            src_ref=src, dst_ref=dst, send_sem=send_sem.at[k], recv_sem=recv_sem.at[k],
            device_id=peer, device_id_type=pl.DeviceIdType.MESH,
        )
        copy.start()
        return copy

    x_own = x_ref[...].reshape(cells, C).astype(jnp.float32)
    mean_own = jnp.sum(x_own, axis=0, keepdims=True) * (1.0 / cells)
    centered_own = x_own - mean_own
    m2_own = jnp.sum(centered_own * centered_own, axis=0, keepdims=True)
    st1[s] = jnp.concatenate([mean_own, m2_own], axis=0)
    xg[j] = x_ref[...]
    cg[pl.ds(F * j, F), pl.ds(1, R)] = c_ref[...]

    pl.semaphore_wait(barrier, len(peers))

    started = []
    s1 = [remote(st1.at[s], st1.at[s], (j, wrap_s(s + d))) for d in range(1, S)]
    cots = []
    for d in range(1, T):
        cots.append(remote(c_ref, cg.at[pl.ds(F * j, F), pl.ds(1, R)], (wrap_j(j + d), s)))
    for d in range(T):
        cots.append(remote(
            c_ref.at[:, pl.ds(R - 1, 1)], cg.at[pl.ds(F * j, F), pl.ds(0, 1)],
            (wrap_j(j + d), wrap_s(s + 1))))
        cots.append(remote(
            c_ref.at[:, pl.ds(0, 1)], cg.at[pl.ds(F * j, F), pl.ds(R + 1, 1)],
            (wrap_j(j + d), wrap_s(s - 1))))
    xs = [remote(x_ref, xg.at[j], (wrap_j(j + d), s)) for d in range(1, T)]
    started += s1 + cots + xs

    def merge(slots, n, count):
        mean = slots[0][0:1]
        for k in range(1, n):
            mean = mean + slots[k][0:1]
        mean = mean * (1.0 / n)
        m2 = jnp.zeros_like(mean)
        for k in range(n):
            delta = slots[k][0:1] - mean
            m2 = m2 + slots[k][1:2] + count * (delta * delta)
        return mean, m2

    for copy in s1:
        copy.wait_recv()
    mean1, m21 = merge(st1, S, float(cells))
    st2[j] = jnp.concatenate([mean1, m21], axis=0)
    s2 = [remote(st2.at[j], st2.at[j], (wrap_j(j + d), s)) for d in range(1, T)]
    started += s2

    for copy in cots:
        copy.wait_recv()
    TF = T * F
    n = TF * (R + 2) * W
    val = cg[...].reshape(n, O).astype(jnp.float32)
    idx = lax.broadcasted_iota(jnp.int32, (n, O), 0)
    col = idx % W
    row = (idx // W) % (R + 2)
    off = ((row == 0) & (s == 0)) | ((row == R + 1) & (s == S - 1))
    val = jnp.where(off, 0.0, val)
    right = jnp.where(col == W - 1, 0.0, pltpu.roll(val, n - 1, 0))
    left = jnp.where(col == 0, 0.0, pltpu.roll(val, 1, 0))
    for c, piece in enumerate((right, val, left)):
        g3[pl.ds(0, TF), :, :, c * O:(c + 1) * O] = piece.astype(jnp.bfloat16).reshape(TF, R + 2, W, O)
    g3[pl.ds(TF, 2)] = jnp.zeros((2, R + 2, W, 3 * O), jnp.bfloat16)

    w_copy.wait()
    total = jnp.zeros((cells, C), jnp.float32)
    for a in range(3):
        for b in range(3):
            block = g3[pl.ds(F * j + 2 - a, F), pl.ds(2 - b, R)].reshape(cells, 3 * O)
            for c in range(3):
                tap = (a * 3 + b) * 3 + c
                total = total + lax.dot_general(
                    block[:, c * O:(c + 1) * O], w_ref[tap * C:(tap + 1) * C],
                    (((1,), (1,)), ((), ())), preferred_element_type=jnp.float32)
    hg[...] = total

    same = (
        lax.broadcasted_iota(jnp.int32, (C, C), 0) // (C // GROUPS)
        == lax.broadcasted_iota(jnp.int32, (C, C), 1) // (C // GROUPS)
    ).astype(jnp.float32)

    def group_sum(v):
        wide = jnp.broadcast_to(v, (8, C))
        return jnp.dot(wide, same, precision=lax.Precision.HIGHEST,
                       preferred_element_type=jnp.float32)[0:1]

    width = C // GROUPS
    channel_count = float(cells * S * T)
    count = channel_count * width
    for copy in s2:
        copy.wait_recv()
    mean2, m22 = merge(st2, T, float(cells * S))
    mean = group_sum(mean2) * (1.0 / width)
    delta = mean2 - mean
    var = group_sum(m22 + channel_count * (delta * delta)) * (1.0 / count)
    inv = lax.rsqrt(var + 1e-06)
    gain = gain_ref[...]
    shift = shift_ref[...]

    for copy in xs:
        copy.wait_recv()
    for k in range(T):
        xk = xg[k].reshape(cells, C).astype(jnp.float32)
        act = (xk - mean) * inv * gain + shift
        hidden = act * jax.nn.sigmoid(act)
        ht[:, k * cells:(k + 1) * cells] = jnp.transpose(hidden).astype(jnp.bfloat16)

    start = jnp.minimum(chunk * j, shard - chunk)
    rows = lambda target: pl.ds(pl.multiple_of(target * shard + start, 32), chunk)
    hidden_t = ht[...]
    pair = []
    for a in range(3):
        for b in range(3):
            g = a * 3 + b
            block = g3[pl.ds(2 - a, TF), pl.ds(2 - b, R)].reshape(T * cells, 3 * O)
            out = jnp.dot(hidden_t, block, preferred_element_type=jnp.float32)
            for c in range(3):
                tap = g * 3 + c
                wg[tap * C:(tap + 1) * C] = out[:, c * O:(c + 1) * O]
            while len(pair) < Z and shard * 2 * (len(pair) + 1) <= 3 * C * (g + 1):
                k = len(pair)
                pair.append(remote(
                    wg.at[rows(2 * k + 1 - core)], pbuf.at[k], (j, 2 * z + 1 - core)))
    started += pair

    normed = (x_own - mean) * inv
    act = normed * gain + shift
    sigma = jax.nn.sigmoid(act)
    act_grad = hg[...] * (sigma * (1.0 + act * (1.0 - sigma)))
    gr1[s] = jnp.concatenate(
        [jnp.sum(act_grad * normed, axis=0, keepdims=True),
         jnp.sum(act_grad, axis=0, keepdims=True)], axis=0)
    g1 = [remote(gr1.at[s], gr1.at[s], (j, wrap_s(s + d))) for d in range(1, S)]
    started += g1
    hg[...] = act_grad

    for copy in pair:
        copy.wait_recv()
    zs = []
    for d in range(1, Z):
        k = lax.rem(z + d, Z)
        sbuf[d - 1] = (wg[rows(2 * k + core)] + pbuf[k]).astype(sbuf.dtype)
        zs.append(remote(sbuf.at[d - 1], rbuf.at[d - 1], (j, 2 * k + core)))
    started += zs

    for copy in g1:
        copy.wait_recv()
    part = gr1[0]
    for k in range(1, S):
        part = part + gr1[k]
    gr2[j] = part
    g2 = [remote(gr2.at[j], gr2.at[j], (wrap_j(j + d), s)) for d in range(1, T)]
    started += g2

    acc = wg[rows(s)] + pbuf[z]
    for d in range(1, Z):
        zs[d - 1].wait_recv()
        acc = acc + rbuf[d - 1].astype(jnp.float32)
    abuf[j] = acc.astype(abuf.dtype)
    ag = [remote(abuf.at[j], abuf.at[j], (wrap_j(j + d), s)) for d in range(1, T)]
    started += ag

    for copy in g2:
        copy.wait_recv()
    sums = gr2[0]
    for k in range(1, T):
        sums = sums + gr2[k]
    gain_grad = sums[0:1]
    shift_grad = sums[1:2]
    gg_ref[...] = gain_grad
    sg_ref[...] = shift_grad
    first = group_sum(gain * shift_grad)
    second = group_sum(gain * gain_grad)
    normed = (x_own - mean) * inv
    clip = inv * (hg[...] * gain - first * (1.0 / count) - normed * (second * (1.0 / count)))
    clip_ref[...] = clip.astype(clip_ref.dtype).reshape(clip_ref.shape)

    for copy in ag:
        copy.wait_recv()
    for k in range(T):
        at = min(chunk * k, shard - chunk)
        wg_out[at:at + chunk] = abuf[k].astype(jnp.float32)
    for copy in started:
        copy.wait_send()


def fused_shards(T, S, latent_clip, cotangent, conv_weight, norm_gain, norm_shift):
    F, R, W, C = latent_clip.shape
    O = cotangent.shape[-1]
    shard = conv_weight.shape[0] // S
    chunk = -(-shard // (T * UNIT)) * UNIT
    cells = F * R * W
    Z = S // 2
    copies = 2 * ((S - 1) + (T - 1)) + 2 * (T - 1) + 2 * T + Z + (Z - 1) + (T - 1)
    vmem = pl.BlockSpec(memory_space=pltpu.VMEM)
    f32, bf16 = jnp.float32, jnp.bfloat16
    clip, wgrad, gg, sg = pl.pallas_call(
        functools.partial(fused_kernel, T, S, shard, chunk),
        out_shape=(
            jax.ShapeDtypeStruct(latent_clip.shape, bf16),
            jax.ShapeDtypeStruct((shard, O), f32),
            jax.ShapeDtypeStruct((1, C), f32),
            jax.ShapeDtypeStruct((1, C), f32),
        ),
        in_specs=[vmem, vmem, pl.BlockSpec(memory_space=pl.ANY), vmem, vmem],
        out_specs=(vmem, vmem, vmem, vmem),
        scratch_shapes=[
            pltpu.VMEM(conv_weight.shape, bf16),
            pltpu.VMEM((T, F, R, W, C), bf16),
            pltpu.VMEM((T * F, R + 2, W, O), bf16),
            pltpu.VMEM((T * F + 2, R + 2, W, 3 * O), bf16),
            pltpu.VMEM((S, 2, C), f32),
            pltpu.VMEM((T, 2, C), f32),
            pltpu.VMEM((S, 2, C), f32),
            pltpu.VMEM((T, 2, C), f32),
            pltpu.VMEM((cells, C), f32),
            pltpu.VMEM((C, T * cells), bf16),
            pltpu.VMEM(conv_weight.shape, f32),
            pltpu.VMEM((Z, chunk, O), f32),
            pltpu.VMEM((Z - 1, chunk, O), bf16),
            pltpu.VMEM((Z - 1, chunk, O), bf16),
            pltpu.VMEM((T, chunk, O), bf16),
            pltpu.SemaphoreType.DMA((copies,)),
            pltpu.SemaphoreType.DMA((copies,)),
            pltpu.SemaphoreType.DMA,
        ],
        compiler_params=pltpu.CompilerParams(
            collective_id=0, has_side_effects=True, vmem_limit_bytes=40 * 1024 * 1024),
    )(latent_clip, cotangent, conv_weight, norm_gain.reshape(1, C), norm_shift.reshape(1, C))
    return clip, wgrad, gg.reshape(C), sg.reshape(C)


def shifted(value, axis, steps):
    count = lax.axis_size(axis)
    leading, last = (max(0, -steps), min(count, count - steps))
    return lax.ppermute(value, axis, [(source, source + steps) for source in range(leading, last)])


def extended_2(block, sides, width):
    for axis, dim in sides:
        count = lax.axis_size(axis)
        forward = [(i, i + 1) for i in range(count - 1)]
        backward = [(target, source) for source, target in forward]
        low = lax.ppermute(
            lax.slice_in_dim(block, block.shape[dim] - width, None, axis=dim), axis, forward
        )
        high = lax.ppermute(lax.slice_in_dim(block, 0, width, axis=dim), axis, backward)
        block = jnp.concatenate([low, block, high], axis=dim)
    return block


def silu_slope(activation):
    sigma = jax.nn.sigmoid(activation)
    return sigma * (1.0 + activation * (1.0 - sigma))


def tap_block(source, anchors, frame_count, row_count, col_count):
    pieces = [
        source[
            anchor[0] : anchor[0] + frame_count,
            anchor[1] : anchor[1] + row_count,
            anchor[2] : anchor[2] + col_count,
            :,
        ]
        for anchor in anchors
    ]
    merged = jnp.concatenate(pieces, axis=-1)
    return merged.reshape(frame_count * row_count * col_count, merged.shape[-1])


def transposed(grad_pad, conv_weight, frame_count, row_count, col_count):
    out_channels = conv_weight.shape[1]
    channels = conv_weight.shape[0] // 27
    kernel = conv_weight.reshape(3, 3, 3, channels, out_channels)
    total = jnp.zeros((frame_count * row_count * col_count, channels), jnp.float32)
    for tap_time in range(3):
        anchors = [
            (2 - tap_time, 2 - tap_row, 2 - tap_col) for tap_row in range(3) for tap_col in range(3)
        ]
        tap_cols = tap_block(grad_pad, anchors, frame_count, row_count, col_count)
        flipped = jnp.transpose(kernel[tap_time], (0, 1, 3, 2)).reshape(9 * out_channels, channels)
        total = total + jnp.dot(tap_cols, flipped, preferred_element_type=jnp.float32)
    return total.reshape(frame_count, row_count, col_count, channels)


def shards(latent_clip, cotangent, conv_weight, norm_gain, norm_shift):
    frame_count, row_count, col_count, channels = latent_clip.shape
    out_channels = cotangent.shape[-1]
    width_group = channels // GROUPS
    tm_size = lax.axis_size("tm")
    space_size = lax.axis_size("space")
    group_count = frame_count * row_count * col_count * width_group * tm_size * space_size
    values = latent_clip.astype(jnp.float32).reshape(
        frame_count, row_count, col_count, GROUPS, width_group
    )
    group_mean = lax.psum(jnp.sum(values, axis=(0, 1, 2, 4)), ("tm", "space")) / group_count
    centered = values - group_mean[:, None]
    group_var = (
        lax.psum(jnp.sum(centered * centered, axis=(0, 1, 2, 4)), ("tm", "space")) / group_count
    )
    inv_std = lax.rsqrt(group_var + 1e-06)
    normed = (centered * inv_std[:, None]).reshape(frame_count, row_count, col_count, channels)
    activation = normed * norm_gain + norm_shift
    hidden = jax.nn.silu(activation).astype(jnp.bfloat16)
    ahead = shifted(cotangent, "tm", -1)
    time_source = jnp.concatenate([cotangent, ahead], axis=0)
    time_pad = (0, 0)
    cached = shifted(hidden, "tm", 1)
    extended = jnp.concatenate([cached, hidden], axis=0)
    rimmed = extended_2(extended, (("space", 1),), 1)
    padded = jnp.pad(rimmed, ((0, 0), (0, 0), (1, 1), (0, 0)))
    cell_count = frame_count * row_count * col_count
    upstream = cotangent.reshape(cell_count, out_channels)
    tap_grads = []
    for tap_time in range(3):
        anchors = [(tap_time, tap_row, tap_col) for tap_row in range(3) for tap_col in range(3)]
        tap_cols = tap_block(padded, anchors, frame_count, row_count, col_count)
        tap_grads.append(
            lax.dot_general(
                tap_cols, upstream, (((0,), (0,)), ((), ())), preferred_element_type=jnp.float32
            )
        )
    local_grad = jnp.concatenate(tap_grads, axis=0)
    space_shard = lax.psum_scatter(local_grad, "space", scatter_dimension=0, tiled=True)
    weight_grad = lax.psum(space_shard, "tm")
    grad_pad = jnp.pad(time_source, (time_pad, (2, 2), (1, 1), (0, 0)))
    spread = transposed(grad_pad, conv_weight, frame_count, row_count + 2, col_count)
    from_below = shifted(spread[:, 0], "space", -1)
    from_above = shifted(spread[:, row_count + 1], "space", 1)
    inner = spread[:, 1 : row_count + 1]
    inner = inner.at[:, row_count - 1].add(from_below)
    inner = inner.at[:, 0].add(from_above)
    activation_grad = inner * silu_slope(activation)
    gain_grad, shift_grad = lax.psum(
        (
            jnp.sum(activation_grad * normed, axis=(0, 1, 2)),
            jnp.sum(activation_grad, axis=(0, 1, 2)),
        ),
        ("tm", "space"),
    )
    first = jnp.sum((norm_gain * shift_grad).reshape(GROUPS, width_group), axis=1)
    second = jnp.sum((norm_gain * gain_grad).reshape(GROUPS, width_group), axis=1)
    scaled = (activation_grad * norm_gain).reshape(
        frame_count, row_count, col_count, GROUPS, width_group
    )
    normed_groups = normed.reshape(frame_count, row_count, col_count, GROUPS, width_group)
    clip_grad = inv_std[:, None] * (
        scaled - first[:, None] / group_count - normed_groups * second[:, None] / group_count
    )
    clip_grad = clip_grad.reshape(frame_count, row_count, col_count, channels).astype(jnp.bfloat16)
    return (clip_grad, weight_grad, gain_grad, shift_grad)


def solution(mesh):
    T, S = mesh.shape["tm"], mesh.shape["space"]

    def block(latent_clip, cotangent, conv_weight, norm_gain, norm_shift):
        rows = conv_weight.shape[0] // S
        aligned = rows % UNIT == 0 and rows >= T * UNIT and S % 2 == 0 and S > 2
        if aligned:
            body = functools.partial(fused_shards, T, S)
        else:
            body = shards
        return body(latent_clip, cotangent, conv_weight, norm_gain, norm_shift)

    return jax.shard_map(
        block,
        mesh=mesh,
        in_specs=(P("tm", "space", None, None), P("tm", "space", None, None), P(), P(), P()),
        out_specs=(P("tm", "space", None, None), P("space", None), P(), P()),
        check_vma=False,
    )
```

```python
import functools

import jax
import jax.numpy as jnp
from jax import lax
from jax.experimental import pallas as pl
from jax.experimental.pallas import tpu as pltpu
from jax.sharding import PartitionSpec as P

GROUPS = 32
UNIT = 32


def fused_kernel(
    T, S, shard, chunk,
    x_hbm, c_hbm, w_hbm, gain_hbm, shift_hbm,
    clip_ref, wg_out, gg_ref, sg_ref,
    gain_ref, shift_ref, w_ref, xg, cg, g3, st1, st2, gr1, gr2, hg, ht, wg, pbuf, sbuf, rbuf, abuf,
    send_sem, recv_sem, zs_sem, zr_sem, load_sem,
):
    F, R, W, C = x_hbm.shape
    O = c_hbm.shape[-1]
    Z = S // 2
    cells = F * R * W
    j = lax.axis_index("tm")
    s = lax.axis_index("space")
    z = s // 2
    core = s % 2
    wrap_s = lambda v: lax.rem(v + S, S)
    wrap_j = lambda v: lax.rem(v + T, T)

    peers = []
    for dj in range(T):
        for ds in range(S):
            if (dj, ds) != (0, 0) and (dj == 0 or ds in (0, 1, S - 1)):
                peers.append((wrap_j(j + dj), wrap_s(s + ds)))
    barrier = pltpu.get_barrier_semaphore()
    for peer in peers:
        pl.semaphore_signal(barrier, inc=1, device_id=peer, device_id_type=pl.DeviceIdType.MESH)

    x_own_ref = xg.at[j]
    c_own_ref = cg.at[pl.ds(F * j, F), pl.ds(1, R)]
    loads = [
        pltpu.make_async_copy(source, target, load_sem.at[k])
        for k, (source, target) in enumerate((
            (x_hbm, x_own_ref), (c_hbm, c_own_ref), (gain_hbm, gain_ref),
            (shift_hbm, shift_ref), (w_hbm, w_ref)))
    ]
    for load in loads:
        load.start()

    counter = [0]
    started = []

    def remote(src, dst, peer):
        k = counter[0]
        counter[0] += 1
        copy = pltpu.make_async_remote_copy(
            src_ref=src, dst_ref=dst, send_sem=send_sem.at[k], recv_sem=recv_sem.at[k],
            device_id=peer, device_id_type=pl.DeviceIdType.MESH,
        )
        copy.start()
        started.append(copy)
        return copy

    loads[0].wait()
    x_own = xg[j].reshape(cells, C).astype(jnp.float32)
    mean_own = jnp.sum(x_own, axis=0, keepdims=True) * (1.0 / cells)
    centered_own = x_own - mean_own
    m2_own = jnp.sum(centered_own * centered_own, axis=0, keepdims=True)
    st1[s] = jnp.concatenate([mean_own, m2_own], axis=0)
    for load in loads[1:4]:
        load.wait()

    pl.semaphore_wait(barrier, len(peers))

    s1 = [remote(st1.at[s], st1.at[s], (j, wrap_s(s + d))) for d in range(1, S)]
    cots = []
    for d in range(1, T):
        cots.append(remote(c_own_ref, c_own_ref, (wrap_j(j + d), s)))
    for d in range(T):
        cots.append(remote(
            cg.at[pl.ds(F * j, F), pl.ds(R, 1)], cg.at[pl.ds(F * j, F), pl.ds(0, 1)],
            (wrap_j(j + d), wrap_s(s + 1))))
        cots.append(remote(
            cg.at[pl.ds(F * j, F), pl.ds(1, 1)], cg.at[pl.ds(F * j, F), pl.ds(R + 1, 1)],
            (wrap_j(j + d), wrap_s(s - 1))))
    xs = [remote(x_own_ref, x_own_ref, (wrap_j(j + d), s)) for d in range(1, T)]

    def merge(slots, n, count):
        mean = slots[0][0:1]
        for k in range(1, n):
            mean = mean + slots[k][0:1]
        mean = mean * (1.0 / n)
        m2 = jnp.zeros_like(mean)
        for k in range(n):
            delta = slots[k][0:1] - mean
            m2 = m2 + slots[k][1:2] + count * (delta * delta)
        return mean, m2

    for copy in s1:
        copy.wait_recv()
    mean1, m21 = merge(st1, S, float(cells))
    st2[j] = jnp.concatenate([mean1, m21], axis=0)
    s2 = [remote(st2.at[j], st2.at[j], (wrap_j(j + d), s)) for d in range(1, T)]

    for copy in cots:
        copy.wait_recv()
    TF = T * F
    n = TF * (R + 2) * W
    val = cg[...].reshape(n, O).astype(jnp.float32)
    idx = lax.broadcasted_iota(jnp.int32, (n, O), 0)
    col = idx % W
    row = (idx // W) % (R + 2)
    off = ((row == 0) & (s == 0)) | ((row == R + 1) & (s == S - 1))
    val = jnp.where(off, 0.0, val)
    right = jnp.where(col == W - 1, 0.0, pltpu.roll(val, n - 1, 0))
    left = jnp.where(col == 0, 0.0, pltpu.roll(val, 1, 0))
    for c, piece in enumerate((right, val, left)):
        g3[pl.ds(0, TF), :, :, c * O:(c + 1) * O] = piece.astype(jnp.bfloat16).reshape(TF, R + 2, W, O)
    g3[pl.ds(TF, 2)] = jnp.zeros((2, R + 2, W, 3 * O), jnp.bfloat16)

    loads[4].wait()
    total = jnp.zeros((cells, C), jnp.float32)
    for a in range(3):
        for b in range(3):
            block = g3[pl.ds(F * j + 2 - a, F), pl.ds(2 - b, R)].reshape(cells, 3 * O)
            for c in range(3):
                tap = (a * 3 + b) * 3 + c
                total = total + lax.dot_general(
                    block[:, c * O:(c + 1) * O], w_ref[tap * C:(tap + 1) * C],
                    (((1,), (1,)), ((), ())), preferred_element_type=jnp.float32)
    hg[...] = total

    same = (
        lax.broadcasted_iota(jnp.int32, (C, C), 0) // (C // GROUPS)
        == lax.broadcasted_iota(jnp.int32, (C, C), 1) // (C // GROUPS)
    ).astype(jnp.float32)

    def group_sum(v):
        wide = jnp.broadcast_to(v, (8, C))
        return jnp.dot(wide, same, precision=lax.Precision.HIGHEST,
                       preferred_element_type=jnp.float32)[0:1]

    width = C // GROUPS
    channel_count = float(cells * S * T)
    count = channel_count * width
    for copy in s2:
        copy.wait_recv()
    mean2, m22 = merge(st2, T, float(cells * S))
    mean = group_sum(mean2) * (1.0 / width)
    delta = mean2 - mean
    var = group_sum(m22 + channel_count * (delta * delta)) * (1.0 / count)
    inv = lax.rsqrt(var + 1e-06)
    gain = gain_ref[...]
    shift = shift_ref[...]

    for copy in xs:
        copy.wait_recv()
    for k in range(T):
        xk = xg[k].reshape(cells, C).astype(jnp.float32)
        act = (xk - mean) * inv * gain + shift
        hidden = act * jax.nn.sigmoid(act)
        ht[:, k * cells:(k + 1) * cells] = jnp.transpose(hidden).astype(jnp.bfloat16)

    start = jnp.minimum(chunk * j, shard - chunk)
    rows = lambda target: pl.ds(pl.multiple_of(target * shard + start, 32), chunk)
    hidden_t = ht[...]
    pair = []

    def across(k):
        return pltpu.make_async_remote_copy(
            src_ref=sbuf.at[k], dst_ref=rbuf.at[z], send_sem=zs_sem.at[k], recv_sem=zr_sem.at[z],
            device_id=(j, 2 * k + core), device_id_type=pl.DeviceIdType.MESH,
        )

    def arriving(k):
        return pltpu.make_async_remote_copy(
            src_ref=sbuf.at[k], dst_ref=rbuf.at[k], send_sem=zs_sem.at[k], recv_sem=zr_sem.at[k],
            device_id=(j, 2 * k + core), device_id_type=pl.DeviceIdType.MESH,
        )

    def forward(k):
        pair[k].wait_recv()

        @pl.when(k != z)
        def _():
            sbuf[k] = (wg[rows(2 * k + core)] + pbuf[k]).astype(sbuf.dtype)
            across(k).start()

    sent = 0
    for a in range(3):
        for b in range(3):
            g = a * 3 + b
            block = g3[pl.ds(2 - a, TF), pl.ds(2 - b, R)].reshape(T * cells, 3 * O)
            out = jnp.dot(hidden_t, block, preferred_element_type=jnp.float32)
            for c in range(3):
                tap = g * 3 + c
                wg[tap * C:(tap + 1) * C] = out[:, c * O:(c + 1) * O]
            while len(pair) < Z and shard * 2 * (len(pair) + 1) <= 3 * C * (g + 1):
                k = len(pair)
                pair.append(remote(
                    wg.at[rows(2 * k + 1 - core)], pbuf.at[k], (j, 2 * z + 1 - core)))
                if k:
                    forward(sent)
                    sent += 1

    normed = (x_own - mean) * inv
    act = normed * gain + shift
    sigma = jax.nn.sigmoid(act)
    act_grad = hg[...] * (sigma * (1.0 + act * (1.0 - sigma)))
    gr1[s] = jnp.concatenate(
        [jnp.sum(act_grad * normed, axis=0, keepdims=True),
         jnp.sum(act_grad, axis=0, keepdims=True)], axis=0)
    g1 = [remote(gr1.at[s], gr1.at[s], (j, wrap_s(s + d))) for d in range(1, S)]
    hg[...] = act_grad

    for k in range(sent, Z):
        forward(k)
    rbuf[z] = jnp.zeros(rbuf.shape[1:], rbuf.dtype)

    for copy in g1:
        copy.wait_recv()
    part = gr1[0]
    for k in range(1, S):
        part = part + gr1[k]
    gr2[j] = part
    g2 = [remote(gr2.at[j], gr2.at[j], (wrap_j(j + d), s)) for d in range(1, T)]

    acc = wg[rows(s)] + pbuf[z]
    for k in range(Z):
        @pl.when(k != z)
        def _():
            arriving(k).wait_recv()
        acc = acc + rbuf[k].astype(jnp.float32)
    abuf[j] = acc.astype(abuf.dtype)
    ag = [remote(abuf.at[j], abuf.at[j], (wrap_j(j + d), s)) for d in range(1, T)]

    for copy in g2:
        copy.wait_recv()
    sums = gr2[0]
    for k in range(1, T):
        sums = sums + gr2[k]
    gain_grad = sums[0:1]
    shift_grad = sums[1:2]
    gg_ref[...] = gain_grad
    sg_ref[...] = shift_grad
    first = group_sum(gain * shift_grad)
    second = group_sum(gain * gain_grad)
    normed = (x_own - mean) * inv
    clip = inv * (hg[...] * gain - first * (1.0 / count) - normed * (second * (1.0 / count)))
    clip_ref[...] = clip.astype(clip_ref.dtype).reshape(clip_ref.shape)

    for copy in ag:
        copy.wait_recv()
    for k in range(T):
        at = min(chunk * k, shard - chunk)
        wg_out[at:at + chunk] = abuf[k].astype(jnp.float32)
    for copy in started:
        copy.wait_send()
    for k in range(Z):
        @pl.when(k != z)
        def _():
            across(k).wait_send()


def store_kernel(*refs):
    count = (len(refs) - 1) // 2
    copies = [
        pltpu.make_async_copy(refs[k], refs[count + k], refs[-1].at[k]) for k in range(count)
    ]
    for copy in copies:
        copy.start()
    for copy in copies:
        copy.wait()


def fused_shards(T, S, latent_clip, cotangent, conv_weight, norm_gain, norm_shift):
    F, R, W, C = latent_clip.shape
    O = cotangent.shape[-1]
    shard = conv_weight.shape[0] // S
    chunk = -(-shard // (T * UNIT)) * UNIT
    cells = F * R * W
    Z = S // 2
    copies = 2 * ((S - 1) + (T - 1)) + 2 * (T - 1) + 2 * T + Z + (T - 1)
    vmem = pl.BlockSpec(memory_space=pltpu.VMEM)
    f32, bf16 = jnp.float32, jnp.bfloat16
    hbm = pl.BlockSpec(memory_space=pl.ANY)
    results = pl.pallas_call(
        functools.partial(fused_kernel, T, S, shard, chunk),
        out_shape=(
            jax.ShapeDtypeStruct(latent_clip.shape, bf16),
            jax.ShapeDtypeStruct((shard, O), f32),
            jax.ShapeDtypeStruct((1, C), f32),
            jax.ShapeDtypeStruct((1, C), f32),
        ),
        in_specs=[hbm] * 5,
        out_specs=(vmem, vmem, vmem, vmem),
        scratch_shapes=[
            pltpu.VMEM((1, C), f32),
            pltpu.VMEM((1, C), f32),
            pltpu.VMEM(conv_weight.shape, bf16),
            pltpu.VMEM((T, F, R, W, C), bf16),
            pltpu.VMEM((T * F, R + 2, W, O), bf16),
            pltpu.VMEM((T * F + 2, R + 2, W, 3 * O), bf16),
            pltpu.VMEM((S, 2, C), f32),
            pltpu.VMEM((T, 2, C), f32),
            pltpu.VMEM((S, 2, C), f32),
            pltpu.VMEM((T, 2, C), f32),
            pltpu.VMEM((cells, C), f32),
            pltpu.VMEM((C, T * cells), bf16),
            pltpu.VMEM(conv_weight.shape, f32),
            pltpu.VMEM((Z, chunk, O), f32),
            pltpu.VMEM((Z, chunk, O), bf16),
            pltpu.VMEM((Z, chunk, O), bf16),
            pltpu.VMEM((T, chunk, O), bf16),
            pltpu.SemaphoreType.DMA((copies,)),
            pltpu.SemaphoreType.DMA((copies,)),
            pltpu.SemaphoreType.DMA((Z,)),
            pltpu.SemaphoreType.DMA((Z,)),
            pltpu.SemaphoreType.DMA((5,)),
        ],
        compiler_params=pltpu.CompilerParams(
            collective_id=0, has_side_effects=True, vmem_limit_bytes=63 * 1024 * 1024),
    )(latent_clip, cotangent, conv_weight, norm_gain.reshape(1, C), norm_shift.reshape(1, C))
    clip, wgrad, gg, sg = pl.pallas_call(
        store_kernel,
        out_shape=tuple(jax.ShapeDtypeStruct(r.shape, r.dtype) for r in results),
        in_specs=[pl.BlockSpec(memory_space=pl.ANY)] * 4,
        out_specs=(pl.BlockSpec(memory_space=pltpu.HBM),) * 4,
        scratch_shapes=[pltpu.SemaphoreType.DMA((4,))],
    )(*results)
    return clip, wgrad, gg.reshape(C), sg.reshape(C)


def shifted(value, axis, steps):
    count = lax.axis_size(axis)
    leading, last = (max(0, -steps), min(count, count - steps))
    return lax.ppermute(value, axis, [(source, source + steps) for source in range(leading, last)])


def extended_2(block, sides, width):
    for axis, dim in sides:
        count = lax.axis_size(axis)
        forward = [(i, i + 1) for i in range(count - 1)]
        backward = [(target, source) for source, target in forward]
        low = lax.ppermute(
            lax.slice_in_dim(block, block.shape[dim] - width, None, axis=dim), axis, forward
        )
        high = lax.ppermute(lax.slice_in_dim(block, 0, width, axis=dim), axis, backward)
        block = jnp.concatenate([low, block, high], axis=dim)
    return block


def silu_slope(activation):
    sigma = jax.nn.sigmoid(activation)
    return sigma * (1.0 + activation * (1.0 - sigma))


def tap_block(source, anchors, frame_count, row_count, col_count):
    pieces = [
        source[
            anchor[0] : anchor[0] + frame_count,
            anchor[1] : anchor[1] + row_count,
            anchor[2] : anchor[2] + col_count,
            :,
        ]
        for anchor in anchors
    ]
    merged = jnp.concatenate(pieces, axis=-1)
    return merged.reshape(frame_count * row_count * col_count, merged.shape[-1])


def transposed(grad_pad, conv_weight, frame_count, row_count, col_count):
    out_channels = conv_weight.shape[1]
    channels = conv_weight.shape[0] // 27
    kernel = conv_weight.reshape(3, 3, 3, channels, out_channels)
    total = jnp.zeros((frame_count * row_count * col_count, channels), jnp.float32)
    for tap_time in range(3):
        anchors = [
            (2 - tap_time, 2 - tap_row, 2 - tap_col) for tap_row in range(3) for tap_col in range(3)
        ]
        tap_cols = tap_block(grad_pad, anchors, frame_count, row_count, col_count)
        flipped = jnp.transpose(kernel[tap_time], (0, 1, 3, 2)).reshape(9 * out_channels, channels)
        total = total + jnp.dot(tap_cols, flipped, preferred_element_type=jnp.float32)
    return total.reshape(frame_count, row_count, col_count, channels)


def shards(latent_clip, cotangent, conv_weight, norm_gain, norm_shift):
    frame_count, row_count, col_count, channels = latent_clip.shape
    out_channels = cotangent.shape[-1]
    width_group = channels // GROUPS
    tm_size = lax.axis_size("tm")
    space_size = lax.axis_size("space")
    group_count = frame_count * row_count * col_count * width_group * tm_size * space_size
    values = latent_clip.astype(jnp.float32).reshape(
        frame_count, row_count, col_count, GROUPS, width_group
    )
    group_mean = lax.psum(jnp.sum(values, axis=(0, 1, 2, 4)), ("tm", "space")) / group_count
    centered = values - group_mean[:, None]
    group_var = (
        lax.psum(jnp.sum(centered * centered, axis=(0, 1, 2, 4)), ("tm", "space")) / group_count
    )
    inv_std = lax.rsqrt(group_var + 1e-06)
    normed = (centered * inv_std[:, None]).reshape(frame_count, row_count, col_count, channels)
    activation = normed * norm_gain + norm_shift
    hidden = jax.nn.silu(activation).astype(jnp.bfloat16)
    ahead = shifted(cotangent, "tm", -1)
    time_source = jnp.concatenate([cotangent, ahead], axis=0)
    time_pad = (0, 0)
    cached = shifted(hidden, "tm", 1)
    extended = jnp.concatenate([cached, hidden], axis=0)
    rimmed = extended_2(extended, (("space", 1),), 1)
    padded = jnp.pad(rimmed, ((0, 0), (0, 0), (1, 1), (0, 0)))
    cell_count = frame_count * row_count * col_count
    upstream = cotangent.reshape(cell_count, out_channels)
    tap_grads = []
    for tap_time in range(3):
        anchors = [(tap_time, tap_row, tap_col) for tap_row in range(3) for tap_col in range(3)]
        tap_cols = tap_block(padded, anchors, frame_count, row_count, col_count)
        tap_grads.append(
            lax.dot_general(
                tap_cols, upstream, (((0,), (0,)), ((), ())), preferred_element_type=jnp.float32
            )
        )
    local_grad = jnp.concatenate(tap_grads, axis=0)
    space_shard = lax.psum_scatter(local_grad, "space", scatter_dimension=0, tiled=True)
    weight_grad = lax.psum(space_shard, "tm")
    grad_pad = jnp.pad(time_source, (time_pad, (2, 2), (1, 1), (0, 0)))
    spread = transposed(grad_pad, conv_weight, frame_count, row_count + 2, col_count)
    from_below = shifted(spread[:, 0], "space", -1)
    from_above = shifted(spread[:, row_count + 1], "space", 1)
    inner = spread[:, 1 : row_count + 1]
    inner = inner.at[:, row_count - 1].add(from_below)
    inner = inner.at[:, 0].add(from_above)
    activation_grad = inner * silu_slope(activation)
    gain_grad, shift_grad = lax.psum(
        (
            jnp.sum(activation_grad * normed, axis=(0, 1, 2)),
            jnp.sum(activation_grad, axis=(0, 1, 2)),
        ),
        ("tm", "space"),
    )
    first = jnp.sum((norm_gain * shift_grad).reshape(GROUPS, width_group), axis=1)
    second = jnp.sum((norm_gain * gain_grad).reshape(GROUPS, width_group), axis=1)
    scaled = (activation_grad * norm_gain).reshape(
        frame_count, row_count, col_count, GROUPS, width_group
    )
    normed_groups = normed.reshape(frame_count, row_count, col_count, GROUPS, width_group)
    clip_grad = inv_std[:, None] * (
        scaled - first[:, None] / group_count - normed_groups * second[:, None] / group_count
    )
    clip_grad = clip_grad.reshape(frame_count, row_count, col_count, channels).astype(jnp.bfloat16)
    return (clip_grad, weight_grad, gain_grad, shift_grad)


def solution(mesh):
    T, S = mesh.shape["tm"], mesh.shape["space"]

    def block(latent_clip, cotangent, conv_weight, norm_gain, norm_shift):
        rows = conv_weight.shape[0] // S
        aligned = rows % UNIT == 0 and rows >= T * UNIT and S % 2 == 0 and S > 2
        if aligned:
            body = functools.partial(fused_shards, T, S)
        else:
            body = shards
        return body(latent_clip, cotangent, conv_weight, norm_gain, norm_shift)

    return jax.shard_map(
        block,
        mesh=mesh,
        in_specs=(P("tm", "space", None, None), P("tm", "space", None, None), P(), P(), P()),
        out_specs=(P("tm", "space", None, None), P("space", None), P(), P()),
        check_vma=False,
    )
```

```python
import functools

import jax
import jax.numpy as jnp
from jax import lax
from jax.experimental import pallas as pl
from jax.experimental.pallas import tpu as pltpu
from jax.sharding import PartitionSpec as P

GROUPS = 32
UNIT = 32


def fused_kernel(
    T, S, shard, chunk,
    x_hbm, c_hbm, w_hbm, gain_hbm, shift_hbm,
    clip_out, parts_out, sums_out,
    gain_ref, shift_ref, w_ref, xg, cg, g3, st1, st2, gr1, gr2, hg, ht, wg, pbuf, sbuf, rbuf, abuf, clip_ref, sums_ref,
    send_sem, recv_sem, zs_sem, zr_sem, load_sem, store_sem,
):
    F, R, W, C = x_hbm.shape
    O = c_hbm.shape[-1]
    Z = S // 2
    cells = F * R * W
    j = lax.axis_index("tm")
    s = lax.axis_index("space")
    z = s // 2
    core = s % 2
    wrap_s = lambda v: lax.rem(v + S, S)
    wrap_j = lambda v: lax.rem(v + T, T)

    peers = []
    for dj in range(T):
        for ds in range(S):
            if (dj, ds) != (0, 0) and (dj == 0 or ds in (0, 1, S - 1)):
                peers.append((wrap_j(j + dj), wrap_s(s + ds)))
    barrier = pltpu.get_barrier_semaphore()
    for peer in peers:
        pl.semaphore_signal(barrier, inc=1, device_id=peer, device_id_type=pl.DeviceIdType.MESH)

    x_own_ref = xg.at[j]
    c_own_ref = cg.at[pl.ds(F * j, F), pl.ds(1, R)]
    loads = [
        pltpu.make_async_copy(source, target, load_sem.at[k])
        for k, (source, target) in enumerate((
            (x_hbm, x_own_ref), (c_hbm, c_own_ref), (gain_hbm, gain_ref),
            (shift_hbm, shift_ref), (w_hbm, w_ref)))
    ]
    for load in loads:
        load.start()

    counter = [0]
    started = []

    def remote(src, dst, peer):
        k = counter[0]
        counter[0] += 1
        copy = pltpu.make_async_remote_copy(
            src_ref=src, dst_ref=dst, send_sem=send_sem.at[k], recv_sem=recv_sem.at[k],
            device_id=peer, device_id_type=pl.DeviceIdType.MESH,
        )
        copy.start()
        started.append(copy)
        return copy

    loads[0].wait()
    x_own = xg[j].reshape(cells, C).astype(jnp.float32)
    mean_own = jnp.sum(x_own, axis=0, keepdims=True) * (1.0 / cells)
    centered_own = x_own - mean_own
    m2_own = jnp.sum(centered_own * centered_own, axis=0, keepdims=True)
    st1[s] = jnp.concatenate([mean_own, m2_own], axis=0)
    for load in loads[1:4]:
        load.wait()

    pl.semaphore_wait(barrier, len(peers))

    s1 = [remote(st1.at[s], st1.at[s], (j, wrap_s(s + d))) for d in range(1, S)]
    xs = [remote(x_own_ref, x_own_ref, (wrap_j(j + d), s)) for d in range(1, T)]
    cots = []
    for d in range(1, T):
        cots.append(remote(c_own_ref, c_own_ref, (wrap_j(j + d), s)))
    for d in range(T):
        cots.append(remote(
            cg.at[pl.ds(F * j, F), pl.ds(R, 1)], cg.at[pl.ds(F * j, F), pl.ds(0, 1)],
            (wrap_j(j + d), wrap_s(s + 1))))
        cots.append(remote(
            cg.at[pl.ds(F * j, F), pl.ds(1, 1)], cg.at[pl.ds(F * j, F), pl.ds(R + 1, 1)],
            (wrap_j(j + d), wrap_s(s - 1))))

    def merge(slots, n, count):
        mean = slots[0][0:1]
        for k in range(1, n):
            mean = mean + slots[k][0:1]
        mean = mean * (1.0 / n)
        m2 = jnp.zeros_like(mean)
        for k in range(n):
            delta = slots[k][0:1] - mean
            m2 = m2 + slots[k][1:2] + count * (delta * delta)
        return mean, m2

    for copy in s1:
        copy.wait_recv()
    mean1, m21 = merge(st1, S, float(cells))
    st2[j] = jnp.concatenate([mean1, m21], axis=0)
    s2 = [remote(st2.at[j], st2.at[j], (wrap_j(j + d), s)) for d in range(1, T)]

    for copy in cots:
        copy.wait_recv()
    TF = T * F
    n = TF * (R + 2) * W
    val = cg[...].reshape(n, O).astype(jnp.float32)
    idx = lax.broadcasted_iota(jnp.int32, (n, O), 0)
    col = idx % W
    row = (idx // W) % (R + 2)
    off = ((row == 0) & (s == 0)) | ((row == R + 1) & (s == S - 1))
    val = jnp.where(off, 0.0, val)
    right = jnp.where(col == W - 1, 0.0, pltpu.roll(val, n - 1, 0))
    left = jnp.where(col == 0, 0.0, pltpu.roll(val, 1, 0))
    for c, piece in enumerate((right, val, left)):
        g3[pl.ds(0, TF), :, :, c * O:(c + 1) * O] = piece.astype(jnp.bfloat16).reshape(TF, R + 2, W, O)
    g3[pl.ds(TF, 2)] = jnp.zeros((2, R + 2, W, 3 * O), jnp.bfloat16)

    loads[4].wait()
    total = jnp.zeros((cells, C), jnp.float32)
    for a in range(3):
        for b in range(3):
            block = g3[pl.ds(F * j + 2 - a, F), pl.ds(2 - b, R)].reshape(cells, 3 * O)
            for c in range(3):
                tap = (a * 3 + b) * 3 + c
                total = total + lax.dot_general(
                    block[:, c * O:(c + 1) * O], w_ref[tap * C:(tap + 1) * C],
                    (((1,), (1,)), ((), ())), preferred_element_type=jnp.float32)
    hg[...] = total

    same = (
        lax.broadcasted_iota(jnp.int32, (C, C), 0) // (C // GROUPS)
        == lax.broadcasted_iota(jnp.int32, (C, C), 1) // (C // GROUPS)
    ).astype(jnp.float32)

    def group_sum(v):
        wide = jnp.broadcast_to(v, (8, C))
        return jnp.dot(wide, same, precision=lax.Precision.HIGHEST,
                       preferred_element_type=jnp.float32)[0:1]

    width = C // GROUPS
    channel_count = float(cells * S * T)
    count = channel_count * width
    for copy in s2:
        copy.wait_recv()
    mean2, m22 = merge(st2, T, float(cells * S))
    mean = group_sum(mean2) * (1.0 / width)
    delta = mean2 - mean
    var = group_sum(m22 + channel_count * (delta * delta)) * (1.0 / count)
    inv = lax.rsqrt(var + 1e-06)
    gain = gain_ref[...]
    shift = shift_ref[...]

    for copy in xs:
        copy.wait_recv()
    for k in range(T):
        xk = xg[k].reshape(cells, C).astype(jnp.float32)
        act = (xk - mean) * inv * gain + shift
        hidden = act * jax.nn.sigmoid(act)
        ht[:, k * cells:(k + 1) * cells] = jnp.transpose(hidden).astype(jnp.bfloat16)

    start = jnp.minimum(chunk * j, shard - chunk)
    rows = lambda target: pl.ds(pl.multiple_of(target * shard + start, 32), chunk)
    hidden_t = ht[...]
    pair = []

    def across(k):
        return pltpu.make_async_remote_copy(
            src_ref=sbuf.at[k], dst_ref=rbuf.at[z], send_sem=zs_sem.at[k], recv_sem=zr_sem.at[z],
            device_id=(j, 2 * k + core), device_id_type=pl.DeviceIdType.MESH,
        )

    def arriving(k):
        return pltpu.make_async_remote_copy(
            src_ref=sbuf.at[k], dst_ref=rbuf.at[k], send_sem=zs_sem.at[k], recv_sem=zr_sem.at[k],
            device_id=(j, 2 * k + core), device_id_type=pl.DeviceIdType.MESH,
        )

    def forward(k):
        pair[k].wait_recv()

        @pl.when(k != z)
        def _():
            sbuf[k] = (wg[rows(2 * k + core)] + pbuf[k]).astype(sbuf.dtype)
            across(k).start()

    sent = 0
    for a in range(3):
        for b in range(3):
            g = a * 3 + b
            block = g3[pl.ds(2 - a, TF), pl.ds(2 - b, R)].reshape(T * cells, 3 * O)
            out = jnp.dot(hidden_t, block, preferred_element_type=jnp.float32)
            for c in range(3):
                tap = g * 3 + c
                wg[tap * C:(tap + 1) * C] = out[:, c * O:(c + 1) * O]
            while len(pair) < Z and shard * 2 * (len(pair) + 1) <= 3 * C * (g + 1):
                k = len(pair)
                pair.append(remote(
                    wg.at[rows(2 * k + 1 - core)], pbuf.at[k], (j, 2 * z + 1 - core)))
                if k:
                    forward(sent)
                    sent += 1

    normed = (x_own - mean) * inv
    act = normed * gain + shift
    sigma = jax.nn.sigmoid(act)
    act_grad = hg[...] * (sigma * (1.0 + act * (1.0 - sigma)))
    gr1[s] = jnp.concatenate(
        [jnp.sum(act_grad * normed, axis=0, keepdims=True),
         jnp.sum(act_grad, axis=0, keepdims=True)], axis=0)
    g1 = [remote(gr1.at[s], gr1.at[s], (j, wrap_s(s + d))) for d in range(1, S)]
    hg[...] = act_grad

    for k in range(sent, Z):
        forward(k)
    rbuf[z] = jnp.zeros(rbuf.shape[1:], rbuf.dtype)

    for copy in g1:
        copy.wait_recv()
    part = gr1[0]
    for k in range(1, S):
        part = part + gr1[k]
    gr2[j] = part
    g2 = [remote(gr2.at[j], gr2.at[j], (wrap_j(j + d), s)) for d in range(1, T)]

    acc = wg[rows(s)] + pbuf[z]
    for k in range(Z):
        @pl.when(k != z)
        def _():
            arriving(k).wait_recv()
        acc = acc + rbuf[k].astype(jnp.float32)
    abuf[j] = acc.astype(abuf.dtype)
    ag = [remote(abuf.at[j], abuf.at[j], (wrap_j(j + d), s)) for d in range(1, T)]

    for copy in g2:
        copy.wait_recv()
    sums = gr2[0]
    for k in range(1, T):
        sums = sums + gr2[k]
    gain_grad = sums[0:1]
    shift_grad = sums[1:2]
    sums_ref[...] = sums
    first = group_sum(gain * shift_grad)
    second = group_sum(gain * gain_grad)
    normed = (x_own - mean) * inv
    clip = inv * (hg[...] * gain - first * (1.0 / count) - normed * (second * (1.0 / count)))
    clip_ref[...] = clip.astype(clip_ref.dtype).reshape(clip_ref.shape)
    stores = [
        pltpu.make_async_copy(source, target, store_sem.at[k])
        for k, (source, target) in enumerate((
            (clip_ref, clip_out), (sums_ref, sums_out), (abuf, parts_out)))
    ]
    stores[0].start()
    stores[1].start()

    for copy in ag:
        copy.wait_recv()
    stores[2].start()
    for copy in started:
        copy.wait_send()
    for k in range(Z):
        @pl.when(k != z)
        def _():
            across(k).wait_send()
    for store in stores:
        store.wait()


def store_kernel(shard, chunk, clip_in, parts_in, sums_in, clip_ref, wg_ref, gg_ref, sg_ref):
    clip_ref[...] = clip_in[...]
    for k in range(parts_in.shape[0]):
        at = min(chunk * k, shard - chunk)
        wg_ref[at:at + chunk] = parts_in[k].astype(jnp.float32)
    gg_ref[...] = sums_in[0:1]
    sg_ref[...] = sums_in[1:2]


def fused_shards(T, S, latent_clip, cotangent, conv_weight, norm_gain, norm_shift):
    F, R, W, C = latent_clip.shape
    O = cotangent.shape[-1]
    shard = conv_weight.shape[0] // S
    chunk = -(-shard // (T * UNIT)) * UNIT
    cells = F * R * W
    Z = S // 2
    copies = 2 * ((S - 1) + (T - 1)) + 2 * (T - 1) + 2 * T + Z + (T - 1)
    vmem = pl.BlockSpec(memory_space=pltpu.VMEM)
    f32, bf16 = jnp.float32, jnp.bfloat16
    hbm = pl.BlockSpec(memory_space=pl.ANY)
    results = pl.pallas_call(
        functools.partial(fused_kernel, T, S, shard, chunk),
        out_shape=(
            jax.ShapeDtypeStruct(latent_clip.shape, bf16),
            jax.ShapeDtypeStruct((T, chunk, O), bf16),
            jax.ShapeDtypeStruct((2, C), f32),
        ),
        in_specs=[hbm] * 5,
        out_specs=(hbm,) * 3,
        scratch_shapes=[
            pltpu.VMEM((1, C), f32),
            pltpu.VMEM((1, C), f32),
            pltpu.VMEM(conv_weight.shape, bf16),
            pltpu.VMEM((T, F, R, W, C), bf16),
            pltpu.VMEM((T * F, R + 2, W, O), bf16),
            pltpu.VMEM((T * F + 2, R + 2, W, 3 * O), bf16),
            pltpu.VMEM((S, 2, C), f32),
            pltpu.VMEM((T, 2, C), f32),
            pltpu.VMEM((S, 2, C), f32),
            pltpu.VMEM((T, 2, C), f32),
            pltpu.VMEM((cells, C), f32),
            pltpu.VMEM((C, T * cells), bf16),
            pltpu.VMEM(conv_weight.shape, f32),
            pltpu.VMEM((Z, chunk, O), f32),
            pltpu.VMEM((Z, chunk, O), bf16),
            pltpu.VMEM((Z, chunk, O), bf16),
            pltpu.VMEM((T, chunk, O), bf16),
            pltpu.VMEM(latent_clip.shape, bf16),
            pltpu.VMEM((2, C), f32),
            pltpu.SemaphoreType.DMA((copies,)),
            pltpu.SemaphoreType.DMA((copies,)),
            pltpu.SemaphoreType.DMA((Z,)),
            pltpu.SemaphoreType.DMA((Z,)),
            pltpu.SemaphoreType.DMA((5,)),
            pltpu.SemaphoreType.DMA((3,)),
        ],
        compiler_params=pltpu.CompilerParams(
            collective_id=0, has_side_effects=True, vmem_limit_bytes=63 * 1024 * 1024),
    )(latent_clip, cotangent, conv_weight, norm_gain.reshape(1, C), norm_shift.reshape(1, C))
    clip, wgrad, gg, sg = pl.pallas_call(
        functools.partial(store_kernel, shard, chunk),
        out_shape=(
            jax.ShapeDtypeStruct(latent_clip.shape, bf16),
            jax.ShapeDtypeStruct((shard, O), f32),
            jax.ShapeDtypeStruct((1, C), f32),
            jax.ShapeDtypeStruct((1, C), f32),
        ),
        in_specs=[vmem] * 3,
        out_specs=(pl.BlockSpec(memory_space=pltpu.VMEM),) * 4,
    )(*results)
    return clip, wgrad, gg.reshape(C), sg.reshape(C)


def shifted(value, axis, steps):
    count = lax.axis_size(axis)
    leading, last = (max(0, -steps), min(count, count - steps))
    return lax.ppermute(value, axis, [(source, source + steps) for source in range(leading, last)])


def extended_2(block, sides, width):
    for axis, dim in sides:
        count = lax.axis_size(axis)
        forward = [(i, i + 1) for i in range(count - 1)]
        backward = [(target, source) for source, target in forward]
        low = lax.ppermute(
            lax.slice_in_dim(block, block.shape[dim] - width, None, axis=dim), axis, forward
        )
        high = lax.ppermute(lax.slice_in_dim(block, 0, width, axis=dim), axis, backward)
        block = jnp.concatenate([low, block, high], axis=dim)
    return block


def silu_slope(activation):
    sigma = jax.nn.sigmoid(activation)
    return sigma * (1.0 + activation * (1.0 - sigma))


def tap_block(source, anchors, frame_count, row_count, col_count):
    pieces = [
        source[
            anchor[0] : anchor[0] + frame_count,
            anchor[1] : anchor[1] + row_count,
            anchor[2] : anchor[2] + col_count,
            :,
        ]
        for anchor in anchors
    ]
    merged = jnp.concatenate(pieces, axis=-1)
    return merged.reshape(frame_count * row_count * col_count, merged.shape[-1])


def transposed(grad_pad, conv_weight, frame_count, row_count, col_count):
    out_channels = conv_weight.shape[1]
    channels = conv_weight.shape[0] // 27
    kernel = conv_weight.reshape(3, 3, 3, channels, out_channels)
    total = jnp.zeros((frame_count * row_count * col_count, channels), jnp.float32)
    for tap_time in range(3):
        anchors = [
            (2 - tap_time, 2 - tap_row, 2 - tap_col) for tap_row in range(3) for tap_col in range(3)
        ]
        tap_cols = tap_block(grad_pad, anchors, frame_count, row_count, col_count)
        flipped = jnp.transpose(kernel[tap_time], (0, 1, 3, 2)).reshape(9 * out_channels, channels)
        total = total + jnp.dot(tap_cols, flipped, preferred_element_type=jnp.float32)
    return total.reshape(frame_count, row_count, col_count, channels)


def shards(latent_clip, cotangent, conv_weight, norm_gain, norm_shift):
    frame_count, row_count, col_count, channels = latent_clip.shape
    out_channels = cotangent.shape[-1]
    width_group = channels // GROUPS
    tm_size = lax.axis_size("tm")
    space_size = lax.axis_size("space")
    group_count = frame_count * row_count * col_count * width_group * tm_size * space_size
    values = latent_clip.astype(jnp.float32).reshape(
        frame_count, row_count, col_count, GROUPS, width_group
    )
    group_mean = lax.psum(jnp.sum(values, axis=(0, 1, 2, 4)), ("tm", "space")) / group_count
    centered = values - group_mean[:, None]
    group_var = (
        lax.psum(jnp.sum(centered * centered, axis=(0, 1, 2, 4)), ("tm", "space")) / group_count
    )
    inv_std = lax.rsqrt(group_var + 1e-06)
    normed = (centered * inv_std[:, None]).reshape(frame_count, row_count, col_count, channels)
    activation = normed * norm_gain + norm_shift
    hidden = jax.nn.silu(activation).astype(jnp.bfloat16)
    ahead = shifted(cotangent, "tm", -1)
    time_source = jnp.concatenate([cotangent, ahead], axis=0)
    time_pad = (0, 0)
    cached = shifted(hidden, "tm", 1)
    extended = jnp.concatenate([cached, hidden], axis=0)
    rimmed = extended_2(extended, (("space", 1),), 1)
    padded = jnp.pad(rimmed, ((0, 0), (0, 0), (1, 1), (0, 0)))
    cell_count = frame_count * row_count * col_count
    upstream = cotangent.reshape(cell_count, out_channels)
    tap_grads = []
    for tap_time in range(3):
        anchors = [(tap_time, tap_row, tap_col) for tap_row in range(3) for tap_col in range(3)]
        tap_cols = tap_block(padded, anchors, frame_count, row_count, col_count)
        tap_grads.append(
            lax.dot_general(
                tap_cols, upstream, (((0,), (0,)), ((), ())), preferred_element_type=jnp.float32
            )
        )
    local_grad = jnp.concatenate(tap_grads, axis=0)
    space_shard = lax.psum_scatter(local_grad, "space", scatter_dimension=0, tiled=True)
    weight_grad = lax.psum(space_shard, "tm")
    grad_pad = jnp.pad(time_source, (time_pad, (2, 2), (1, 1), (0, 0)))
    spread = transposed(grad_pad, conv_weight, frame_count, row_count + 2, col_count)
    from_below = shifted(spread[:, 0], "space", -1)
    from_above = shifted(spread[:, row_count + 1], "space", 1)
    inner = spread[:, 1 : row_count + 1]
    inner = inner.at[:, row_count - 1].add(from_below)
    inner = inner.at[:, 0].add(from_above)
    activation_grad = inner * silu_slope(activation)
    gain_grad, shift_grad = lax.psum(
        (
            jnp.sum(activation_grad * normed, axis=(0, 1, 2)),
            jnp.sum(activation_grad, axis=(0, 1, 2)),
        ),
        ("tm", "space"),
    )
    first = jnp.sum((norm_gain * shift_grad).reshape(GROUPS, width_group), axis=1)
    second = jnp.sum((norm_gain * gain_grad).reshape(GROUPS, width_group), axis=1)
    scaled = (activation_grad * norm_gain).reshape(
        frame_count, row_count, col_count, GROUPS, width_group
    )
    normed_groups = normed.reshape(frame_count, row_count, col_count, GROUPS, width_group)
    clip_grad = inv_std[:, None] * (
        scaled - first[:, None] / group_count - normed_groups * second[:, None] / group_count
    )
    clip_grad = clip_grad.reshape(frame_count, row_count, col_count, channels).astype(jnp.bfloat16)
    return (clip_grad, weight_grad, gain_grad, shift_grad)


def solution(mesh):
    T, S = mesh.shape["tm"], mesh.shape["space"]

    def block(latent_clip, cotangent, conv_weight, norm_gain, norm_shift):
        rows = conv_weight.shape[0] // S
        aligned = rows % UNIT == 0 and rows >= T * UNIT and S % 2 == 0 and S > 2
        if aligned:
            body = functools.partial(fused_shards, T, S)
        else:
            body = shards
        return body(latent_clip, cotangent, conv_weight, norm_gain, norm_shift)

    return jax.shard_map(
        block,
        mesh=mesh,
        in_specs=(P("tm", "space", None, None), P("tm", "space", None, None), P(), P(), P()),
        out_specs=(P("tm", "space", None, None), P("space", None), P(), P()),
        check_vma=False,
    )
```

```python
import functools

import jax
import jax.numpy as jnp
from jax import lax
from jax.experimental import pallas as pl
from jax.experimental.pallas import tpu as pltpu
from jax.sharding import PartitionSpec as P

GROUPS = 32
UNIT = 32


def fused_kernel(
    T, S, shard, chunk,
    x_hbm, c_hbm, w_hbm, gain_hbm, shift_hbm,
    clip_out, parts_out, sums_out,
    gain_ref, shift_ref, w_ref, xg, cg, g3, st1, st2, gr1, gr2, hg, ht, wg, pbuf, sbuf, rbuf, abuf, clip_ref, sums_ref,
    send_sem, recv_sem, zs_sem, zr_sem, load_sem, store_sem,
):
    F, R, W, C = x_hbm.shape
    O = c_hbm.shape[-1]
    Z = S // 2
    cells = F * R * W
    j = lax.axis_index("tm")
    s = lax.axis_index("space")
    z = s // 2
    core = s % 2
    wrap_s = lambda v: lax.rem(v + S, S)
    wrap_j = lambda v: lax.rem(v + T, T)

    peers = []
    for dj in range(T):
        for ds in range(S):
            if (dj, ds) != (0, 0) and (dj == 0 or ds in (0, 1, S - 1)):
                peers.append((wrap_j(j + dj), wrap_s(s + ds)))
    barrier = pltpu.get_barrier_semaphore()
    for peer in peers:
        pl.semaphore_signal(barrier, inc=1, device_id=peer, device_id_type=pl.DeviceIdType.MESH)

    x_own_ref = xg.at[j]
    c_own_ref = cg.at[pl.ds(F * j, F), pl.ds(1, R)]
    loads = [
        pltpu.make_async_copy(source, target, load_sem.at[k])
        for k, (source, target) in enumerate((
            (x_hbm, x_own_ref), (c_hbm, c_own_ref), (gain_hbm, gain_ref),
            (shift_hbm, shift_ref), (w_hbm, w_ref)))
    ]
    for load in loads:
        load.start()

    counter = [0]
    started = []

    def remote(src, dst, peer):
        k = counter[0]
        counter[0] += 1
        copy = pltpu.make_async_remote_copy(
            src_ref=src, dst_ref=dst, send_sem=send_sem.at[k], recv_sem=recv_sem.at[k],
            device_id=peer, device_id_type=pl.DeviceIdType.MESH,
        )
        copy.start()
        started.append(copy)
        return copy

    loads[0].wait()
    x_own = xg[j].reshape(cells, C).astype(jnp.float32)
    mean_own = jnp.sum(x_own, axis=0, keepdims=True) * (1.0 / cells)
    centered_own = x_own - mean_own
    m2_own = jnp.sum(centered_own * centered_own, axis=0, keepdims=True)
    st1[s] = jnp.concatenate([mean_own, m2_own], axis=0)
    for load in loads[1:4]:
        load.wait()

    pl.semaphore_wait(barrier, len(peers))

    s1 = [remote(st1.at[s], st1.at[s], (j, wrap_s(s + d))) for d in range(1, S)]
    xs = [remote(x_own_ref, x_own_ref, (wrap_j(j + d), s)) for d in range(1, T)]
    cots = []
    for d in range(1, T):
        cots.append(remote(c_own_ref, c_own_ref, (wrap_j(j + d), s)))
    for d in range(T):
        cots.append(remote(
            cg.at[pl.ds(F * j, F), pl.ds(R, 1)], cg.at[pl.ds(F * j, F), pl.ds(0, 1)],
            (wrap_j(j + d), wrap_s(s + 1))))
        cots.append(remote(
            cg.at[pl.ds(F * j, F), pl.ds(1, 1)], cg.at[pl.ds(F * j, F), pl.ds(R + 1, 1)],
            (wrap_j(j + d), wrap_s(s - 1))))

    def merge(slots, n, count):
        mean = slots[0][0:1]
        for k in range(1, n):
            mean = mean + slots[k][0:1]
        mean = mean * (1.0 / n)
        m2 = jnp.zeros_like(mean)
        for k in range(n):
            delta = slots[k][0:1] - mean
            m2 = m2 + slots[k][1:2] + count * (delta * delta)
        return mean, m2

    for copy in s1:
        copy.wait_recv()
    mean1, m21 = merge(st1, S, float(cells))
    st2[j] = jnp.concatenate([mean1, m21], axis=0)
    s2 = [remote(st2.at[j], st2.at[j], (wrap_j(j + d), s)) for d in range(1, T)]

    for copy in cots:
        copy.wait_recv()
    TF = T * F
    n = TF * (R + 2) * W
    val = cg[...].reshape(n, O).astype(jnp.float32)
    idx = lax.broadcasted_iota(jnp.int32, (n, O), 0)
    col = idx % W
    row = (idx // W) % (R + 2)
    off = ((row == 0) & (s == 0)) | ((row == R + 1) & (s == S - 1))
    val = jnp.where(off, 0.0, val)
    right = jnp.where(col == W - 1, 0.0, pltpu.roll(val, n - 1, 0))
    left = jnp.where(col == 0, 0.0, pltpu.roll(val, 1, 0))
    for c, piece in enumerate((right, val, left)):
        g3[pl.ds(0, TF), :, :, c * O:(c + 1) * O] = piece.astype(jnp.bfloat16).reshape(TF, R + 2, W, O)
    g3[pl.ds(TF, 2)] = jnp.zeros((2, R + 2, W, 3 * O), jnp.bfloat16)

    loads[4].wait()
    total = jnp.zeros((cells, C), jnp.float32)
    for a in range(3):
        for b in range(3):
            block = g3[pl.ds(F * j + 2 - a, F), pl.ds(2 - b, R)].reshape(cells, 3 * O)
            for c in range(3):
                tap = (a * 3 + b) * 3 + c
                total = total + lax.dot_general(
                    block[:, c * O:(c + 1) * O], w_ref[tap * C:(tap + 1) * C],
                    (((1,), (1,)), ((), ())), preferred_element_type=jnp.float32)
    hg[...] = total

    same = (
        lax.broadcasted_iota(jnp.int32, (C, C), 0) // (C // GROUPS)
        == lax.broadcasted_iota(jnp.int32, (C, C), 1) // (C // GROUPS)
    ).astype(jnp.float32)

    def group_sum(v):
        wide = jnp.broadcast_to(v, (8, C))
        return jnp.dot(wide, same, precision=lax.Precision.HIGHEST,
                       preferred_element_type=jnp.float32)[0:1]

    width = C // GROUPS
    channel_count = float(cells * S * T)
    count = channel_count * width
    for copy in s2:
        copy.wait_recv()
    mean2, m22 = merge(st2, T, float(cells * S))
    mean = group_sum(mean2) * (1.0 / width)
    delta = mean2 - mean
    var = group_sum(m22 + channel_count * (delta * delta)) * (1.0 / count)
    inv = lax.rsqrt(var + 1e-06)
    gain = gain_ref[...]
    shift = shift_ref[...]

    normed = (x_own - mean) * inv
    act = normed * gain + shift
    sigma = jax.nn.sigmoid(act)
    act_grad = hg[...] * (sigma * (1.0 + act * (1.0 - sigma)))
    gr1[s] = jnp.concatenate(
        [jnp.sum(act_grad * normed, axis=0, keepdims=True),
         jnp.sum(act_grad, axis=0, keepdims=True)], axis=0)
    g1 = [remote(gr1.at[s], gr1.at[s], (j, wrap_s(s + d))) for d in range(1, S)]
    hg[...] = act_grad

    for copy in xs:
        copy.wait_recv()
    for k in range(T):
        xk = xg[k].reshape(cells, C).astype(jnp.float32)
        act = (xk - mean) * inv * gain + shift
        hidden = act * jax.nn.sigmoid(act)
        ht[:, k * cells:(k + 1) * cells] = jnp.transpose(hidden).astype(jnp.bfloat16)

    start = jnp.minimum(chunk * j, shard - chunk)
    rows = lambda target: pl.ds(pl.multiple_of(target * shard + start, 32), chunk)
    hidden_t = ht[...]
    pair = []

    def across(k):
        return pltpu.make_async_remote_copy(
            src_ref=sbuf.at[k], dst_ref=rbuf.at[z], send_sem=zs_sem.at[k], recv_sem=zr_sem.at[z],
            device_id=(j, 2 * k + core), device_id_type=pl.DeviceIdType.MESH,
        )

    def arriving(k):
        return pltpu.make_async_remote_copy(
            src_ref=sbuf.at[k], dst_ref=rbuf.at[k], send_sem=zs_sem.at[k], recv_sem=zr_sem.at[k],
            device_id=(j, 2 * k + core), device_id_type=pl.DeviceIdType.MESH,
        )

    def forward(k):
        pair[k].wait_recv()

        @pl.when(k != z)
        def _():
            sbuf[k] = (wg[rows(2 * k + core)] + pbuf[k]).astype(sbuf.dtype)
            across(k).start()

    sent = 0
    for a in range(3):
        for b in range(3):
            g = a * 3 + b
            block = g3[pl.ds(2 - a, TF), pl.ds(2 - b, R)].reshape(T * cells, 3 * O)
            out = jnp.dot(hidden_t, block, preferred_element_type=jnp.float32)
            for c in range(3):
                tap = g * 3 + c
                wg[tap * C:(tap + 1) * C] = out[:, c * O:(c + 1) * O]
            if g == 4:
                for copy in g1:
                    copy.wait_recv()
                part = gr1[0]
                for k in range(1, S):
                    part = part + gr1[k]
                gr2[j] = part
                g2 = [remote(gr2.at[j], gr2.at[j], (wrap_j(j + d), s)) for d in range(1, T)]
            while len(pair) < Z and shard * 2 * (len(pair) + 1) <= 3 * C * (g + 1):
                k = len(pair)
                pair.append(remote(
                    wg.at[rows(2 * k + 1 - core)], pbuf.at[k], (j, 2 * z + 1 - core)))
                if k:
                    forward(sent)
                    sent += 1

    for k in range(sent, Z):
        forward(k)
    rbuf[z] = jnp.zeros(rbuf.shape[1:], rbuf.dtype)

    for copy in g2:
        copy.wait_recv()
    sums = gr2[0]
    for k in range(1, T):
        sums = sums + gr2[k]
    gain_grad = sums[0:1]
    shift_grad = sums[1:2]
    sums_ref[...] = sums
    first = group_sum(gain * shift_grad)
    second = group_sum(gain * gain_grad)
    normed = (x_own - mean) * inv
    clip = inv * (hg[...] * gain - first * (1.0 / count) - normed * (second * (1.0 / count)))
    clip_ref[...] = clip.astype(clip_ref.dtype).reshape(clip_ref.shape)
    stores = [
        pltpu.make_async_copy(source, target, store_sem.at[k])
        for k, (source, target) in enumerate((
            (clip_ref, clip_out), (sums_ref, sums_out), (abuf, parts_out)))
    ]
    stores[0].start()
    stores[1].start()

    for copy in started:
        copy.wait_send()

    acc = wg[rows(s)] + pbuf[z]
    for k in range(Z):
        @pl.when(k != z)
        def _():
            arriving(k).wait_recv()
        acc = acc + rbuf[k].astype(jnp.float32)
    abuf[j] = acc.astype(abuf.dtype)
    ag = [remote(abuf.at[j], abuf.at[j], (wrap_j(j + d), s)) for d in range(1, T)]

    for k in range(Z):
        @pl.when(k != z)
        def _():
            across(k).wait_send()

    for copy in ag:
        copy.wait_recv()
    stores[2].start()
    for copy in ag:
        copy.wait_send()
    for store in stores:
        store.wait()


def store_kernel(shard, chunk, clip_in, parts_in, sums_in, clip_ref, wg_ref, gg_ref, sg_ref):
    clip_ref[...] = clip_in[...]
    for k in range(parts_in.shape[0]):
        at = min(chunk * k, shard - chunk)
        wg_ref[at:at + chunk] = parts_in[k].astype(jnp.float32)
    gg_ref[...] = sums_in[0:1]
    sg_ref[...] = sums_in[1:2]


def fused_shards(T, S, latent_clip, cotangent, conv_weight, norm_gain, norm_shift):
    F, R, W, C = latent_clip.shape
    O = cotangent.shape[-1]
    shard = conv_weight.shape[0] // S
    chunk = -(-shard // (T * UNIT)) * UNIT
    cells = F * R * W
    Z = S // 2
    copies = 2 * ((S - 1) + (T - 1)) + 2 * (T - 1) + 2 * T + Z + (T - 1)
    vmem = pl.BlockSpec(memory_space=pltpu.VMEM)
    f32, bf16 = jnp.float32, jnp.bfloat16
    hbm = pl.BlockSpec(memory_space=pl.ANY)
    results = pl.pallas_call(
        functools.partial(fused_kernel, T, S, shard, chunk),
        out_shape=(
            jax.ShapeDtypeStruct(latent_clip.shape, bf16),
            jax.ShapeDtypeStruct((T, chunk, O), bf16),
            jax.ShapeDtypeStruct((2, C), f32),
        ),
        in_specs=[hbm] * 5,
        out_specs=(hbm,) * 3,
        scratch_shapes=[
            pltpu.VMEM((1, C), f32),
            pltpu.VMEM((1, C), f32),
            pltpu.VMEM(conv_weight.shape, bf16),
            pltpu.VMEM((T, F, R, W, C), bf16),
            pltpu.VMEM((T * F, R + 2, W, O), bf16),
            pltpu.VMEM((T * F + 2, R + 2, W, 3 * O), bf16),
            pltpu.VMEM((S, 2, C), f32),
            pltpu.VMEM((T, 2, C), f32),
            pltpu.VMEM((S, 2, C), f32),
            pltpu.VMEM((T, 2, C), f32),
            pltpu.VMEM((cells, C), f32),
            pltpu.VMEM((C, T * cells), bf16),
            pltpu.VMEM(conv_weight.shape, f32),
            pltpu.VMEM((Z, chunk, O), f32),
            pltpu.VMEM((Z, chunk, O), bf16),
            pltpu.VMEM((Z, chunk, O), bf16),
            pltpu.VMEM((T, chunk, O), bf16),
            pltpu.VMEM(latent_clip.shape, bf16),
            pltpu.VMEM((2, C), f32),
            pltpu.SemaphoreType.DMA((copies,)),
            pltpu.SemaphoreType.DMA((copies,)),
            pltpu.SemaphoreType.DMA((Z,)),
            pltpu.SemaphoreType.DMA((Z,)),
            pltpu.SemaphoreType.DMA((5,)),
            pltpu.SemaphoreType.DMA((3,)),
        ],
        compiler_params=pltpu.CompilerParams(
            collective_id=0, has_side_effects=True, vmem_limit_bytes=63 * 1024 * 1024),
    )(latent_clip, cotangent, conv_weight, norm_gain.reshape(1, C), norm_shift.reshape(1, C))
    clip, wgrad, gg, sg = pl.pallas_call(
        functools.partial(store_kernel, shard, chunk),
        out_shape=(
            jax.ShapeDtypeStruct(latent_clip.shape, bf16),
            jax.ShapeDtypeStruct((shard, O), f32),
            jax.ShapeDtypeStruct((1, C), f32),
            jax.ShapeDtypeStruct((1, C), f32),
        ),
        in_specs=[vmem] * 3,
        out_specs=(pl.BlockSpec(memory_space=pltpu.VMEM),) * 4,
    )(*results)
    return clip, wgrad, gg.reshape(C), sg.reshape(C)


def shifted(value, axis, steps):
    count = lax.axis_size(axis)
    leading, last = (max(0, -steps), min(count, count - steps))
    return lax.ppermute(value, axis, [(source, source + steps) for source in range(leading, last)])


def extended_2(block, sides, width):
    for axis, dim in sides:
        count = lax.axis_size(axis)
        forward = [(i, i + 1) for i in range(count - 1)]
        backward = [(target, source) for source, target in forward]
        low = lax.ppermute(
            lax.slice_in_dim(block, block.shape[dim] - width, None, axis=dim), axis, forward
        )
        high = lax.ppermute(lax.slice_in_dim(block, 0, width, axis=dim), axis, backward)
        block = jnp.concatenate([low, block, high], axis=dim)
    return block


def silu_slope(activation):
    sigma = jax.nn.sigmoid(activation)
    return sigma * (1.0 + activation * (1.0 - sigma))


def tap_block(source, anchors, frame_count, row_count, col_count):
    pieces = [
        source[
            anchor[0] : anchor[0] + frame_count,
            anchor[1] : anchor[1] + row_count,
            anchor[2] : anchor[2] + col_count,
            :,
        ]
        for anchor in anchors
    ]
    merged = jnp.concatenate(pieces, axis=-1)
    return merged.reshape(frame_count * row_count * col_count, merged.shape[-1])


def transposed(grad_pad, conv_weight, frame_count, row_count, col_count):
    out_channels = conv_weight.shape[1]
    channels = conv_weight.shape[0] // 27
    kernel = conv_weight.reshape(3, 3, 3, channels, out_channels)
    total = jnp.zeros((frame_count * row_count * col_count, channels), jnp.float32)
    for tap_time in range(3):
        anchors = [
            (2 - tap_time, 2 - tap_row, 2 - tap_col) for tap_row in range(3) for tap_col in range(3)
        ]
        tap_cols = tap_block(grad_pad, anchors, frame_count, row_count, col_count)
        flipped = jnp.transpose(kernel[tap_time], (0, 1, 3, 2)).reshape(9 * out_channels, channels)
        total = total + jnp.dot(tap_cols, flipped, preferred_element_type=jnp.float32)
    return total.reshape(frame_count, row_count, col_count, channels)


def shards(latent_clip, cotangent, conv_weight, norm_gain, norm_shift):
    frame_count, row_count, col_count, channels = latent_clip.shape
    out_channels = cotangent.shape[-1]
    width_group = channels // GROUPS
    tm_size = lax.axis_size("tm")
    space_size = lax.axis_size("space")
    group_count = frame_count * row_count * col_count * width_group * tm_size * space_size
    values = latent_clip.astype(jnp.float32).reshape(
        frame_count, row_count, col_count, GROUPS, width_group
    )
    group_mean = lax.psum(jnp.sum(values, axis=(0, 1, 2, 4)), ("tm", "space")) / group_count
    centered = values - group_mean[:, None]
    group_var = (
        lax.psum(jnp.sum(centered * centered, axis=(0, 1, 2, 4)), ("tm", "space")) / group_count
    )
    inv_std = lax.rsqrt(group_var + 1e-06)
    normed = (centered * inv_std[:, None]).reshape(frame_count, row_count, col_count, channels)
    activation = normed * norm_gain + norm_shift
    hidden = jax.nn.silu(activation).astype(jnp.bfloat16)
    ahead = shifted(cotangent, "tm", -1)
    time_source = jnp.concatenate([cotangent, ahead], axis=0)
    time_pad = (0, 0)
    cached = shifted(hidden, "tm", 1)
    extended = jnp.concatenate([cached, hidden], axis=0)
    rimmed = extended_2(extended, (("space", 1),), 1)
    padded = jnp.pad(rimmed, ((0, 0), (0, 0), (1, 1), (0, 0)))
    cell_count = frame_count * row_count * col_count
    upstream = cotangent.reshape(cell_count, out_channels)
    tap_grads = []
    for tap_time in range(3):
        anchors = [(tap_time, tap_row, tap_col) for tap_row in range(3) for tap_col in range(3)]
        tap_cols = tap_block(padded, anchors, frame_count, row_count, col_count)
        tap_grads.append(
            lax.dot_general(
                tap_cols, upstream, (((0,), (0,)), ((), ())), preferred_element_type=jnp.float32
            )
        )
    local_grad = jnp.concatenate(tap_grads, axis=0)
    space_shard = lax.psum_scatter(local_grad, "space", scatter_dimension=0, tiled=True)
    weight_grad = lax.psum(space_shard, "tm")
    grad_pad = jnp.pad(time_source, (time_pad, (2, 2), (1, 1), (0, 0)))
    spread = transposed(grad_pad, conv_weight, frame_count, row_count + 2, col_count)
    from_below = shifted(spread[:, 0], "space", -1)
    from_above = shifted(spread[:, row_count + 1], "space", 1)
    inner = spread[:, 1 : row_count + 1]
    inner = inner.at[:, row_count - 1].add(from_below)
    inner = inner.at[:, 0].add(from_above)
    activation_grad = inner * silu_slope(activation)
    gain_grad, shift_grad = lax.psum(
        (
            jnp.sum(activation_grad * normed, axis=(0, 1, 2)),
            jnp.sum(activation_grad, axis=(0, 1, 2)),
        ),
        ("tm", "space"),
    )
    first = jnp.sum((norm_gain * shift_grad).reshape(GROUPS, width_group), axis=1)
    second = jnp.sum((norm_gain * gain_grad).reshape(GROUPS, width_group), axis=1)
    scaled = (activation_grad * norm_gain).reshape(
        frame_count, row_count, col_count, GROUPS, width_group
    )
    normed_groups = normed.reshape(frame_count, row_count, col_count, GROUPS, width_group)
    clip_grad = inv_std[:, None] * (
        scaled - first[:, None] / group_count - normed_groups * second[:, None] / group_count
    )
    clip_grad = clip_grad.reshape(frame_count, row_count, col_count, channels).astype(jnp.bfloat16)
    return (clip_grad, weight_grad, gain_grad, shift_grad)


def solution(mesh):
    T, S = mesh.shape["tm"], mesh.shape["space"]

    def block(latent_clip, cotangent, conv_weight, norm_gain, norm_shift):
        rows = conv_weight.shape[0] // S
        aligned = rows % UNIT == 0 and rows >= T * UNIT and S % 2 == 0 and S > 2
        if aligned:
            body = functools.partial(fused_shards, T, S)
        else:
            body = shards
        return body(latent_clip, cotangent, conv_weight, norm_gain, norm_shift)

    return jax.shard_map(
        block,
        mesh=mesh,
        in_specs=(P("tm", "space", None, None), P("tm", "space", None, None), P(), P(), P()),
        out_specs=(P("tm", "space", None, None), P("space", None), P(), P()),
        check_vma=False,
    )
```
